512 devices in a mesh: resp: 32 (over y, z_hi), head: 16 (over z_lo, x, core).
Axes of the slice: x: 4, y: 8, z: 8 (z_hi: 4, z_lo: 2; z = z_hi * 2 + z_lo), core: 2. Of those that a mesh axis runs over, the one named last changes fastest.
Arguments:
- queries: bfloat16 [3072, 8192], P('resp', 'head'), may hold values from -5 to 5
- response_key_value: bfloat16 [3072, 2048], P('resp', 'head'), may hold values from -5 to 5
- prompt_key_value: bfloat16 [1024, 2048], P('resp', 'head'), may hold values from -5 to 5
- output_cotangent: bfloat16 [3072, 8192], P('resp', 'head'), may hold values from -5 to 5
- lengths: int32 [16], replicated, may hold values from 1 to 512, 3072 in all
Outputs:
- attended: bfloat16 [3072, 8192], P('resp', 'head')
- query_gradient: bfloat16 [3072, 8192], P('resp', 'head')
- response_key_value_gradient: bfloat16 [3072, 2048], P('resp', 'head')
- prompt_key_value_gradient: bfloat16 [1024, 2048], P('resp', 'head')
The draws below stay inside these ranges and needn't reach their ends.
Inputs may be any that keep to these rules, and one draw needn't show every extreme that they name: The lengths sum to 3072, and the largest equals 512.
All inputs are finite; a program needn't handle non-finite values.
Results may differ from the reference program's by a relative error of at most 0.028.
Values may be sent and summed in bfloat16 or wider, within the bound.
A program may use at most 64 MiB of HBM per device.

```python
import math
import jax
import jax.numpy as jnp
import numpy as np
from jax import lax

HEAD_SIZE = 128
QUERY_PER_KV = 8
MAXLEN = 512
RESPONSES = 16
ROWS_DEV = 96
KEY_VALUE_HEADS = 8
HQ = 64
PROMPT_ROWS = 1024
PACKED_TOKENS = 3072
DEPTH = 6


def draw_queries(key, part):
    key = jax.random.fold_in(key, 11)
    random_seed_key = jax.random.fold_in(key, 0)
    value_matrix = jnp.clip(1.5 * jax.random.normal(random_seed_key, (PACKED_TOKENS, HQ * HEAD_SIZE), jnp.float32), -5.0, 5.0)
    return value_matrix.astype(jnp.bfloat16)


def draw_prompt_key_value(key, part):
    key = jax.random.fold_in(key, 23)
    random_seed_key = jax.random.fold_in(key, 0)
    value_matrix = jnp.clip(1.5 * jax.random.normal(random_seed_key, (PROMPT_ROWS, KEY_VALUE_HEADS, 2, HEAD_SIZE), jnp.float32), -5.0, 5.0)
    return value_matrix.reshape(PROMPT_ROWS, KEY_VALUE_HEADS * 2 * HEAD_SIZE).astype(jnp.bfloat16)


def steps_of(stream_key, extent, cuts, low, top_value):
    def one(position, parts):
        heights = jax.random.uniform(jax.random.fold_in(jax.random.fold_in(stream_key, 6), position), (parts,), jnp.float32, low / len(cuts), top_value / len(cuts))
        return jnp.repeat(jnp.exp(heights), extent[position] // parts).reshape((-1,) + (1,) * (len(extent) - position - 1))

    level = one(*cuts[0])
    for cut in cuts[1:]:
        level = level * one(*cut)
    return level


def profile(number_of, total, bound, slope):
    loads = [(1 << 20) // math.isqrt(rank ** slope) + 1 for rank in range(2, number_of + 1)]
    spare, given = total - bound - (number_of - 1), [1] * (number_of - 1)
    while spare > 0:
        candidates = [i for i in range(number_of - 1) if given[i] < bound]
        pool, budget = sum([loads[i] for i in candidates]), spare
        for i in candidates:
            addition = min(bound - given[i], max(1, budget * loads[i] // pool), spare)
            given[i] = given[i] + addition
            spare = spare - addition
    return np.array([bound] + given)


def ragged(rng, count, total, bound, slope):
    if count == 2:
        one = jax.random.randint(rng, (), max(1, total - bound), min(bound, total - 1) + 1)
        return jnp.stack([one, total - one])
    tallies = jnp.asarray(profile(count, total, bound, slope), jnp.int32)
    pairs = (count - 1) // 2
    donor, receiver = tallies[1:1 + 2 * pairs:2], tallies[2:2 + 2 * pairs:2]
    slack = jnp.minimum(donor - 1, bound - receiver)
    moved = jax.random.randint(jax.random.fold_in(rng, 1), (pairs,), 0, 1 << 20) % (slack + 1)
    tallies = tallies.at[1:1 + 2 * pairs:2].set(donor - moved).at[2:2 + 2 * pairs:2].set(receiver + moved)
    return tallies[jax.random.permutation(jax.random.fold_in(rng, 2), count)]


def gaussian(stream_key, shape, deviation, bound, cuts=(), kind=jnp.bfloat16):
    drawn = deviation * jax.random.normal(stream_key, shape, jnp.float32)
    if cuts:
        drawn = drawn * steps_of(stream_key, shape, cuts, -0.22, 0.18)
    return jnp.clip(drawn, -bound, bound).astype(kind)


def setup_inputs(seed: int = 0) -> dict:
    splits = jax.random.split(jax.random.key(seed), 6)
    queries = draw_queries(jax.random.fold_in(splits[5], 71), 0)
    response_key_value = gaussian(splits[1], (PACKED_TOKENS, 2 * KEY_VALUE_HEADS * HEAD_SIZE), 1.5, 5.0, ((0, 32), (1, 16)))
    prompt_key_value = draw_prompt_key_value(jax.random.fold_in(splits[5], 71), 0)
    output_cotangent = gaussian(splits[3], (PACKED_TOKENS, HQ * HEAD_SIZE), 1.0, 5.0, ((0, 32), (1, 16)))
    lengths = ragged(splits[4], RESPONSES, PACKED_TOKENS, MAXLEN, 2).astype(jnp.int32)
    return {"queries": queries, "response_key_value": response_key_value, "prompt_key_value": prompt_key_value, "output_cotangent": output_cotangent, "lengths": lengths}


def row_starts(lengths, row_ids):
    bounds = jnp.cumsum(lengths).astype(jnp.int32)
    before = (bounds[None, :] <= row_ids[:, None]).astype(jnp.int32)
    return lax.optimization_barrier(jnp.sum(before * lengths[None, :], axis=1)).astype(jnp.int32)

def reference(queries, response_key_value, prompt_key_value, output_cotangent, lengths):
    logit_scale_factor = 1.0 / math.sqrt(HEAD_SIZE)
    blocks = PACKED_TOKENS // ROWS_DEV
    window_rows = (DEPTH + 1) * ROWS_DEV
    margin = DEPTH * ROWS_DEV
    row_ids = jnp.arange(PACKED_TOKENS, dtype=jnp.int32)
    starts = row_starts(lengths, row_ids)
    padded_ids = jnp.arange(blocks, dtype=jnp.int32)[:, None] * ROWS_DEV + jnp.arange(window_rows, dtype=jnp.int32)[None, :]
    key_ids = padded_ids - margin
    row_grid = row_ids.reshape(blocks, ROWS_DEV)
    start_grid = starts.reshape(blocks, ROWS_DEV)
    allowed = (key_ids[:, None, :] >= start_grid[:, :, None]) & (key_ids[:, None, :] <= row_grid[:, :, None])
    flat_ids = padded_ids.reshape(-1)
    query_head_list = jnp.transpose(queries.reshape(PACKED_TOKENS, KEY_VALUE_HEADS, QUERY_PER_KV, HEAD_SIZE), (1, 2, 0, 3))
    gradient_head_list = jnp.transpose(output_cotangent.reshape(PACKED_TOKENS, KEY_VALUE_HEADS, QUERY_PER_KV, HEAD_SIZE), (1, 2, 0, 3))
    prompt_key_value_pairs = jnp.transpose(prompt_key_value.reshape(PROMPT_ROWS, KEY_VALUE_HEADS, 2, HEAD_SIZE), (1, 0, 2, 3))
    response_key_value_pairs = jnp.transpose(response_key_value.reshape(PACKED_TOKENS, KEY_VALUE_HEADS, 2, HEAD_SIZE), (1, 0, 2, 3))

    def kv_head(inputs):
        group_queries, group_grads, prompt_pair, resp_pair = inputs
        prompt_keys = prompt_pair[:, 0]
        prompt_values = prompt_pair[:, 1]
        zero_rows = jnp.zeros((margin, HEAD_SIZE), jnp.float32)
        span_key_rows = jnp.concatenate([zero_rows, resp_pair[:, 0].astype(jnp.float32)], axis=0)[padded_ids]
        span_value_rows = jnp.concatenate([zero_rows, resp_pair[:, 1].astype(jnp.float32)], axis=0)[padded_ids]

        def one_head(carried, head_inputs):
            key_prompt, value_prompt, key_span_rows, value_span_rows = carried
            query_head, grad_head = head_inputs
            query_block_list = query_head.astype(jnp.float32).reshape(blocks, ROWS_DEV, HEAD_SIZE)
            gradient_block_list = grad_head.astype(jnp.float32).reshape(blocks, ROWS_DEV, HEAD_SIZE)
            prompt_scores = jnp.dot(query_head, prompt_keys.T, preferred_element_type=jnp.float32) * logit_scale_factor
            response_score_matrix = jnp.einsum('qye,qoe->qyo', query_block_list, span_key_rows) * logit_scale_factor
            response_score_matrix = jnp.where(allowed, response_score_matrix, -jnp.inf)
            highest = jnp.maximum(lax.optimization_barrier(jnp.max(prompt_scores, axis=1)), lax.optimization_barrier(jnp.max(response_score_matrix, axis=2)).reshape(PACKED_TOKENS))
            high_grid = highest.reshape(blocks, ROWS_DEV)
            totals = lax.optimization_barrier(jnp.sum(jnp.exp(prompt_scores - highest[:, None]), axis=1))
            totals = totals + lax.optimization_barrier(jnp.sum(jnp.exp(response_score_matrix - high_grid[:, :, None]), axis=2)).reshape(PACKED_TOKENS)
            logsum = highest + jnp.log(totals)
            log_grid = logsum.reshape(blocks, ROWS_DEV)
            prompt_weights = jnp.exp(prompt_scores - logsum[:, None])
            self_weights = jnp.exp(response_score_matrix - log_grid[:, :, None])
            prompt_rounded = prompt_weights.astype(jnp.bfloat16)
            response_weights_rounded = self_weights.astype(jnp.bfloat16)
            attention_output = jnp.dot(prompt_rounded, prompt_values, preferred_element_type=jnp.float32)
            attention_output = attention_output + jnp.einsum('qol,qlt->qot', response_weights_rounded.astype(jnp.float32), span_value_rows).reshape(PACKED_TOKENS, HEAD_SIZE)
            attention_output = attention_output.astype(jnp.bfloat16)
            delta = lax.optimization_barrier(jnp.sum(grad_head.astype(jnp.float32) * attention_output.astype(jnp.float32), axis=1))
            delta_grid = delta.reshape(blocks, ROWS_DEV)
            prompt_dweight = jnp.dot(grad_head, prompt_values.T, preferred_element_type=jnp.float32)
            prompt_dscore = (prompt_weights * (prompt_dweight - delta[:, None])).astype(jnp.bfloat16)
            response_weight_gradient = jnp.einsum('qye,qoe->qyo', gradient_block_list, span_value_rows)
            response_score_gradient = (self_weights * (response_weight_gradient - delta_grid[:, :, None])).astype(jnp.bfloat16)
            query_gradient = jnp.dot(prompt_dscore, prompt_keys, preferred_element_type=jnp.float32)
            query_gradient = query_gradient + jnp.einsum('qol,qlt->qot', response_score_gradient.astype(jnp.float32), span_key_rows).reshape(PACKED_TOKENS, HEAD_SIZE)
            query_gradient = (query_gradient * logit_scale_factor).astype(jnp.bfloat16)
            key_prompt = key_prompt + jnp.dot(prompt_dscore.T, query_head, preferred_element_type=jnp.float32) * logit_scale_factor
            value_prompt = value_prompt + jnp.dot(prompt_rounded.T, grad_head, preferred_element_type=jnp.float32)
            key_span_rows = key_span_rows + jnp.einsum('scp,scx->spx', response_score_gradient.astype(jnp.float32), query_block_list) * logit_scale_factor
            value_span_rows = value_span_rows + jnp.einsum('scp,scx->spx', response_weights_rounded.astype(jnp.float32), gradient_block_list)
            return ((key_prompt, value_prompt, key_span_rows, value_span_rows), (attention_output, query_gradient))
        initial = (jnp.zeros((PROMPT_ROWS, HEAD_SIZE), jnp.float32), jnp.zeros((PROMPT_ROWS, HEAD_SIZE), jnp.float32), jnp.zeros((blocks, window_rows, HEAD_SIZE), jnp.float32), jnp.zeros((blocks, window_rows, HEAD_SIZE), jnp.float32))
        sums, per_head = lax.scan(one_head, initial, (group_queries, group_grads))
        key_prompt, value_prompt, key_span_rows, value_span_rows = sums
        key_resp = jax.ops.segment_sum(key_span_rows.reshape(-1, HEAD_SIZE), flat_ids, num_segments=PACKED_TOKENS + margin)[margin:]
        value_resp = jax.ops.segment_sum(value_span_rows.reshape(-1, HEAD_SIZE), flat_ids, num_segments=PACKED_TOKENS + margin)[margin:]
        return (per_head[0], per_head[1], jnp.stack([key_resp, value_resp], axis=1), jnp.stack([key_prompt, value_prompt], axis=1))
    outputs, query_grads, response_gradient_parts, prompt_gradient_parts = lax.map(kv_head, (query_head_list, gradient_head_list, prompt_key_value_pairs, response_key_value_pairs))
    attended = jnp.transpose(outputs, (2, 0, 1, 3)).reshape(PACKED_TOKENS, HQ * HEAD_SIZE)
    query_gradient = jnp.transpose(query_grads, (2, 0, 1, 3)).reshape(PACKED_TOKENS, HQ * HEAD_SIZE)
    response_key_value_gradient = jnp.transpose(response_gradient_parts, (1, 0, 2, 3)).reshape(PACKED_TOKENS, 2 * KEY_VALUE_HEADS * HEAD_SIZE).astype(jnp.bfloat16)
    prompt_key_value_gradient = jnp.transpose(prompt_gradient_parts, (1, 0, 2, 3)).reshape(PROMPT_ROWS, 2 * KEY_VALUE_HEADS * HEAD_SIZE).astype(jnp.bfloat16)
    return (attended, query_gradient, response_key_value_gradient, prompt_key_value_gradient)
```

```python
import functools
import math

import jax
import jax.numpy as jnp
from jax import lax
from jax.experimental import pallas as pl
from jax.experimental.pallas import tpu as pltpu
from jax.sharding import PartitionSpec as P

MAXLEN = 512
GROUP = 4
MESH = pl.DeviceIdType.MESH
F32 = jnp.float32
BF16 = jnp.bfloat16


def dot(a, b, ca, cb):
    return lax.dot_general(a, b, (((ca,), (cb,)), ((), ())), preferred_element_type=F32)


def wait_bytes(ref, sem):
    pltpu.make_async_copy(ref, ref, sem).wait()


def kernel(
    count,
    q_hbm, kv_hbm, pkv_hbm, do_hbm, len_ref,
    att_hbm, dq_hbm, dkv_hbm, dpkv_hbm,
    qs, dos, kvp, kvw, ebuf, dpbuf, mbuf, wbuf, dsbuf,
    gp, gpin, gpout, rs, gw, gwin, gwout, wr, os, dqs, dkvs, dpkvs,
    load_sem, kv_sem, p_send, p_recv, pf_send, pf_recv, w_send, w_recv, wf_send, wf_recv,
    gx_send, gx_recv, gwx_send, gwx_recv, rs_send, rs_recv, wr_send, wr_recv, out_sem,
):
    rows, width = q_hbm.shape
    d = kv_hbm.shape[1]
    heads = width // d
    cols = heads * rows
    plocal = pkv_hbm.shape[0]
    groups = count // GROUP
    chunk = GROUP * plocal
    reach = kvw.shape[1] // rows - 1
    scale = 1.0 / math.sqrt(d)
    to_log2 = scale * math.log2(math.e)

    me = lax.axis_index("resp")
    head = lax.axis_index("head")
    kind = lax.rem(head, 2)
    other = 1 - kind
    mate = {"head": head + 1 - 2 * kind}
    my_group = me // GROUP
    my_place = lax.rem(me, GROUP)

    def peer(by):
        return lax.rem(me + by + count, count)

    def remote(src, dst, send, recv, to):
        copy = pltpu.make_async_remote_copy(
            src_ref=src, dst_ref=dst, send_sem=send, recv_sem=recv, device_id=to, device_id_type=MESH
        )
        copy.start()

    def prompt_rows(index, size):
        return pl.ds(pl.multiple_of(index * size, size), size)

    own_p = prompt_rows(me, plocal)
    own_w = pl.ds(reach * rows, rows)
    kv_copy = pltpu.make_async_copy(kv_hbm, kvw.at[kind, own_w], kv_sem.at[0])
    pkv_copy = pltpu.make_async_copy(pkv_hbm, kvp.at[kind, own_p], kv_sem.at[1])
    kv_copy.start()
    pkv_copy.start()
    for h in range(heads):
        pltpu.make_async_copy(
            q_hbm.at[:, pl.ds(h * d, d)], qs.at[pl.ds(h * rows, rows)], load_sem.at[0]
        ).start()
        pltpu.make_async_copy(
            do_hbm.at[:, pl.ds(h * d, d)], dos.at[pl.ds(h * rows, rows)], load_sem.at[1]
        ).start()

    barrier = pltpu.get_barrier_semaphore()
    pl.semaphore_signal(barrier, inc=1, device_id=mate, device_id_type=MESH)
    for by in range(1, count):
        pl.semaphore_signal(barrier, inc=1, device_id={"resp": peer(by)}, device_id_type=MESH)
    pl.semaphore_wait(barrier, count)

    kv_copy.wait()
    pkv_copy.wait()
    remote(kvw.at[kind, own_w], kvw.at[kind, own_w], wf_send, wf_recv.at[reach], mate)
    for by in range(1, count):
        remote(
            kvp.at[kind, own_p], kvp.at[kind, own_p], p_send, p_recv.at[my_group],
            {"resp": peer(by)},
        )
    for off in range(1, reach + 1):
        slot = reach - off
        remote(
            kvw.at[kind, own_w], kvw.at[kind, pl.ds(slot * rows, rows)], w_send, w_recv.at[slot],
            {"resp": peer(off)},
        )

    lane = lax.broadcasted_iota(jnp.int32, (1, cols), 1)
    row_id = lane
    for h in range(1, heads):
        row_id = row_id - jnp.where(lane >= h * rows, rows, 0)
    row_id = row_id + me * rows
    start = jnp.zeros((1, cols), jnp.int32)
    bound = jnp.int32(0)
    for j in range(len_ref.shape[0]):
        length = len_ref[j]
        bound = bound + length
        start = start + jnp.where(bound <= row_id, length, 0)

    wait_bytes(qs, load_sem.at[0])
    wait_bytes(dos, load_sem.at[1])

    stats = [None, None, None]

    def forward(index, keys, values, base, size, off=None):
        s = dot(keys, qs[...], 1, 1) * to_log2
        if off is not None:
            key_id = lax.broadcasted_iota(jnp.int32, (size, cols), 0) + (me - off) * rows
            allowed = key_id >= start
            if off == 0:
                allowed = allowed & (key_id <= row_id)
            s = jnp.where(allowed, s, -jnp.inf)
        dp = dot(values, dos[...], 1, 1)
        high = jnp.max(s, axis=0, keepdims=True)
        if stats[0] is not None:
            high = jnp.maximum(high, stats[0])
        e = jnp.exp2(s - high)
        total = jnp.sum(e, axis=0, keepdims=True)
        weighted = jnp.sum(e * dp, axis=0, keepdims=True)
        if stats[0] is not None:
            shrink = jnp.exp2(stats[0] - high)
            total = total + stats[1] * shrink
            weighted = weighted + stats[2] * shrink
        stats[0], stats[1], stats[2] = high, total, weighted
        ebuf[base, :] = e
        dpbuf[base, :] = dp
        mbuf[index] = jnp.broadcast_to(high, (8, cols))

    total_p = groups * chunk

    def group_at(n):
        return lax.rem(my_group + n, groups)

    def w_rows(slot):
        return pl.ds(slot * rows, rows)

    def e_w_rows(slot):
        return pl.ds(total_p + slot * rows, rows)

    wait_bytes(kvw.at[other, own_w], wf_recv.at[reach])
    forward(groups + reach, kvw[0, own_w], kvw[1, own_w], e_w_rows(reach), rows, 0)

    order = sorted(range(groups), key=lambda n: min(n, groups - n))
    steps = [("p", n) for n in order] + [("w", s) for s in range(reach - 1, -1, -1)]

    def forward_step(step):
        what, n = step
        if what == "p":
            g = group_at(n)
            at = prompt_rows(g, chunk)
            wait_bytes(kvp.at[other, at], pf_recv.at[g])
            forward(g, kvp[0, at], kvp[1, at], at, chunk)
        else:
            wait_bytes(kvw.at[other, w_rows(n)], wf_recv.at[n])
            forward(groups + n, kvw[0, w_rows(n)], kvw[1, w_rows(n)], e_w_rows(n), rows, reach - n)

    before = None
    for step in steps:
        what, n = step
        if what == "p":
            g = group_at(n)
            at = prompt_rows(g, chunk)
            got = (GROUP - 1 if n == 0 else GROUP) * plocal
            wait_bytes(kvp.at[kind, pl.ds(0, got)], p_recv.at[g])
            remote(kvp.at[kind, at], kvp.at[kind, at], pf_send, pf_recv.at[g], mate)
        else:
            wait_bytes(kvw.at[kind, w_rows(n)], w_recv.at[n])
            remote(kvw.at[kind, w_rows(n)], kvw.at[kind, w_rows(n)], wf_send, wf_recv.at[n], mate)
        if before is not None:
            forward_step(before)
        before = step
    forward_step(before)

    high, total, weighted = stats
    inverse = 1.0 / total
    delta = weighted * inverse

    def backward(index, base):
        factor = jnp.exp2(mbuf[index][:1] - high) * inverse
        w = ebuf[base, :] * factor
        wb = w.astype(BF16)
        ds = (w * (dpbuf[base, :] - delta)).astype(BF16)
        wbuf[base, :] = wb
        dsbuf[base, :] = ds
        return dot(ds, qs[...], 1, 0) * scale, dot(wb, dos[...], 1, 0)

    def finish_prompt(n):
        g = group_at(n)
        at = prompt_rows(g, chunk)
        wait_bytes(gpin.at[at], gx_recv.at[g])
        gpout[at, :] = (gp[kind, at].astype(F32) + gpin[at, :].astype(F32)).astype(BF16)
        for k in range(1 if n == 0 else 0, GROUP):
            to = g * GROUP + lax.rem(my_place + k, GROUP)
            remote(
                gpout.at[prompt_rows(to, plocal)], rs.at[me], rs_send, rs_recv, {"resp": to}
            )
        if n == 0:
            rs[me] = gpout[own_p, :]

    def finish_window(s):
        wait_bytes(gwin.at[s], gwx_recv.at[s])
        both = gw[kind, s].astype(F32) + gwin[s].astype(F32)
        if s == reach:
            return both
        gwout[s] = both.astype(BF16)
        off = reach - s
        remote(gwout.at[s], wr.at[off - 1], wr_send, wr_recv.at[off - 1], {"resp": peer(-off)})
        return None

    def backward_step(step):
        what, n = step
        if what == "p":
            g = group_at(n)
            at = prompt_rows(g, chunk)
            dk, dv = backward(g, at)
            gp[0, at] = dk.astype(BF16)
            gp[1, at] = dv.astype(BF16)
            remote(gp.at[other, at], gpin.at[at], gx_send, gx_recv.at[g], mate)
        else:
            dk, dv = backward(groups + n, e_w_rows(n))
            gw[0, n] = dk.astype(BF16)
            gw[1, n] = dv.astype(BF16)
            remote(gw.at[other, n], gwin.at[n], gwx_send, gwx_recv.at[n], mate)

    def finish(step):
        return finish_prompt(step[1]) if step[0] == "p" else finish_window(step[1])

    back = [("w", s) for s in range(reach)] + [("p", n) for n in reversed(order)] + [("w", reach)]
    before = None
    for step in back:
        backward_step(step)
        if before is not None:
            finish(before)
        before = step

    values_p = kvp[1]
    values_w = kvw[1]
    p_part = pl.ds(0, total_p)
    w_part = pl.ds(total_p, (reach + 1) * rows)
    out_t = dot(values_p, wbuf[p_part, :], 0, 0) + dot(values_w, wbuf[w_part, :], 0, 0)
    os[...] = out_t.T.astype(BF16)
    own_grad = finish(before)
    for h in range(heads):
        pltpu.make_async_copy(
            os.at[pl.ds(h * rows, rows)], att_hbm.at[:, pl.ds(h * d, d)], out_sem.at[0]
        ).start()
    dq_t = dot(kvp[0], dsbuf[p_part, :], 0, 0) + dot(kvw[0], dsbuf[w_part, :], 0, 0)
    dqs[...] = (dq_t.T * scale).astype(BF16)
    for h in range(heads):
        pltpu.make_async_copy(
            dqs.at[pl.ds(h * rows, rows)], dq_hbm.at[:, pl.ds(h * d, d)], out_sem.at[1]
        ).start()

    for off in range(1, reach + 1):
        wait_bytes(wr.at[off - 1], wr_recv.at[off - 1])
        own_grad = own_grad + wr[off - 1].astype(F32)
    dkvs[...] = own_grad.astype(BF16)
    dkv_copy = pltpu.make_async_copy(dkvs, dkv_hbm, out_sem.at[2])
    dkv_copy.start()
    wait_bytes(rs.at[pl.ds(0, count - 1)], rs_recv)
    dpkvs[...] = jnp.sum(rs[...].astype(F32), axis=0).astype(BF16)
    dpkv_copy = pltpu.make_async_copy(dpkvs, dpkv_hbm, out_sem.at[3])
    dpkv_copy.start()

    wait_bytes(kvp.at[0, pl.ds(0, (count - 1) * plocal)], p_send)
    wait_bytes(kvp.at[0], pf_send)
    wait_bytes(kvw.at[0, pl.ds(0, reach * rows)], w_send)
    wait_bytes(kvw.at[0], wf_send)
    wait_bytes(gpin, gx_send)
    wait_bytes(gwin, gwx_send)
    wait_bytes(rs.at[pl.ds(0, count - 1)], rs_send)
    wait_bytes(wr, wr_send)
    wait_bytes(os, out_sem.at[0])
    wait_bytes(dqs, out_sem.at[1])
    dkv_copy.wait()
    dpkv_copy.wait()


def shards(queries, response_key_value, prompt_key_value, output_cotangent, lengths):
    rows, width = queries.shape
    d = response_key_value.shape[1]
    cols = width // d * rows
    plocal = prompt_key_value.shape[0]
    count = lax.axis_size("resp")
    total_p = plocal * count
    groups = count // GROUP
    reach = (MAXLEN + rows - 2) // rows
    keys = total_p + (reach + 1) * rows
    dma, anywhere = pltpu.SemaphoreType.DMA, pl.BlockSpec(memory_space=pl.ANY)
    return pl.pallas_call(
        functools.partial(kernel, count),
        out_shape=(
            jax.ShapeDtypeStruct(queries.shape, BF16),
            jax.ShapeDtypeStruct(queries.shape, BF16),
            jax.ShapeDtypeStruct(response_key_value.shape, BF16),
            jax.ShapeDtypeStruct(prompt_key_value.shape, BF16),
        ),
        in_specs=[anywhere] * 4 + [pl.BlockSpec(memory_space=pltpu.SMEM)],
        out_specs=(anywhere,) * 4,
        scratch_shapes=[
            pltpu.VMEM((cols, d), BF16),
            pltpu.VMEM((cols, d), BF16),
            pltpu.VMEM((2, total_p, d), BF16),
            pltpu.VMEM((2, (reach + 1) * rows, d), BF16),
            pltpu.VMEM((keys, cols), F32),
            pltpu.VMEM((keys, cols), F32),
            pltpu.VMEM((groups + reach + 1, 8, cols), F32),
            pltpu.VMEM((keys, cols), BF16),
            pltpu.VMEM((keys, cols), BF16),
            pltpu.VMEM((2, total_p, d), BF16),
            pltpu.VMEM((total_p, d), BF16),
            pltpu.VMEM((total_p, d), BF16),
            pltpu.VMEM((count, plocal, d), BF16),
            pltpu.VMEM((2, reach + 1, rows, d), BF16),
            pltpu.VMEM((reach + 1, rows, d), BF16),
            pltpu.VMEM((reach, rows, d), BF16),
            pltpu.VMEM((reach, rows, d), BF16),
            pltpu.VMEM((cols, d), BF16),
            pltpu.VMEM((cols, d), BF16),
            pltpu.VMEM((rows, d), BF16),
            pltpu.VMEM((plocal, d), BF16),
            dma((2,)), dma((2,)),
            dma, dma((groups,)), dma, dma((groups,)),
            dma, dma((reach,)), dma, dma((reach + 1,)),
            dma, dma((groups,)), dma, dma((reach + 1,)),
            dma, dma, dma, dma((reach,)),
            dma((4,)),
        ],
        compiler_params=pltpu.CompilerParams(
            collective_id=0, has_side_effects=True, vmem_limit_bytes=40 * 1024 * 1024
        ),
    )(queries, response_key_value, prompt_key_value, output_cotangent, lengths)


def solution(mesh):
    spec = P("resp", "head")
    return jax.shard_map(
        shards,
        mesh=mesh,
        in_specs=(spec, spec, spec, spec, P()),
        out_specs=(spec, spec, spec, spec),
        check_vma=False,
    )
```

```python
import functools
import math

import jax
import jax.numpy as jnp
from jax import lax
from jax.experimental import pallas as pl
from jax.experimental.pallas import tpu as pltpu
from jax.sharding import PartitionSpec as P

MAXLEN = 512
GROUP = 4
AHEAD = 4
BEHIND = 5
MESH = pl.DeviceIdType.MESH
F32 = jnp.float32
BF16 = jnp.bfloat16


def dot(a, b, ca, cb):
    return lax.dot_general(a, b, (((ca,), (cb,)), ((), ())), preferred_element_type=F32)


def wait_bytes(ref, sem):
    pltpu.make_async_copy(ref, ref, sem).wait()


def copy_to(src, dst, send, recv, to):
    pltpu.make_async_remote_copy(
        src_ref=src, dst_ref=dst, send_sem=send, recv_sem=recv, device_id=to, device_id_type=MESH
    ).start()


def at(index, size):
    return pl.ds(pl.multiple_of(index * size, size), size)


def copy_kernel(*refs):
    half = len(refs) // 2
    for i in range(half):
        refs[half + i][...] = refs[i][...]


def window_shape(rows):
    reach = (MAXLEN + rows - 2) // rows
    return reach, -(-(MAXLEN - 1 - (reach - 1) * rows) // 16) * 16


def kernel(
    count,
    q_hbm, kv_hbm, pkv_hbm, do_hbm, len_ref,
    att_hbm, dq_hbm, dkv_hbm, dpkv_hbm,
    qs, dos, kvp, kvw, ebuf, dpbuf, mbuf, wbuf, dsbuf,
    gp, gpin, gpout, rs, gw, gwin, gwout, wr, os, dqs, dkvs, dpkvs,
    load_sem, kv_sem, one_send, a_piece, b_piece, two_send, a_recv, b_recv, pf_send, pf_recv,
    w_send, w_recv, wf_send, wf_recv,
    gx_send, gx_recv, gwx_send, gwx_recv, rs_send, rs_recv, wr_send, wr_recv, out_sem,
):
    rows, width = q_hbm.shape
    d = kv_hbm.shape[1]
    heads = width // d
    cols = heads * rows
    plocal = pkv_hbm.shape[0]
    ny = count // GROUP
    size_a = ny // 2 * plocal
    size_b = GROUP // 2 * plocal
    total_p = count * plocal
    reach, tail = window_shape(rows)
    ahead = tail + (reach - 1) * rows
    scale = 1.0 / math.sqrt(d)
    to_log2 = scale * math.log2(math.e)

    me = lax.axis_index("resp")
    head = lax.axis_index("head")
    kind = lax.rem(head, 2)
    other = 1 - kind
    mate = {"head": head + 1 - 2 * kind}
    y, z = me // GROUP, lax.rem(me, GROUP)

    def device(by, bz):
        return {"resp": lax.rem(y + by, ny) * GROUP + lax.rem(z + bz, GROUP)}

    def peer(by):
        return {"resp": lax.rem(me + by + count, count)}

    odd = lax.rem(y + z, 2)
    own_index = (1 - odd) * (z * (ny // 2) + y // 2) + odd * (
        GROUP * (ny // 2) + y * (GROUP // 2) + z // 2
    )
    own_p = at(own_index, plocal)

    def part_a(pz):
        return at(pz, size_a)

    def part_b(py):
        return pl.ds(pl.multiple_of(GROUP * size_a + py * size_b, size_b), size_b)

    def block(off):
        if off == reach:
            return pl.ds(0, tail)
        return pl.ds(tail + (reach - 1 - off) * rows, rows)

    own_w = block(0)
    z_order = (1, 3, 2)
    y_order = sorted(range(1, ny), key=lambda by: min(by, ny - by))

    kv_copy = pltpu.make_async_copy(kv_hbm, kvw.at[kind, own_w], kv_sem)
    kv_copy.start()

    @pl.when(odd == 0)
    def _():
        pltpu.make_async_copy(pkv_hbm, kvp.at[kind, own_p], a_piece).start()

    @pl.when(odd == 1)
    def _():
        pltpu.make_async_copy(pkv_hbm, kvp.at[kind, own_p], b_piece).start()

    for h in range(heads):
        pltpu.make_async_copy(
            q_hbm.at[:, pl.ds(h * d, d)], qs.at[pl.ds(h * rows, rows)], load_sem.at[0]
        ).start()
        pltpu.make_async_copy(
            do_hbm.at[:, pl.ds(h * d, d)], dos.at[pl.ds(h * rows, rows)], load_sem.at[1]
        ).start()

    barrier = pltpu.get_barrier_semaphore()
    pl.semaphore_signal(barrier, inc=1, device_id=mate, device_id_type=MESH)
    for by in range(1, count):
        pl.semaphore_signal(barrier, inc=1, device_id=peer(by), device_id_type=MESH)
    pl.semaphore_wait(barrier, count)

    @pl.when(odd == 0)
    def _():
        for by in y_order:
            copy_to(pkv_hbm, kvp.at[kind, own_p], one_send.at[0], a_piece, device(by, 0))

    @pl.when(odd == 1)
    def _():
        for bz in z_order:
            copy_to(pkv_hbm, kvp.at[kind, own_p], one_send.at[1], b_piece, device(0, bz))

    kv_copy.wait()
    copy_to(kvw.at[kind, own_w], kvw.at[kind, own_w], wf_send, wf_recv.at[0], mate)
    for off in range(1, reach + 1):
        size = tail if off == reach else rows
        copy_to(
            kvw.at[kind, pl.ds(ahead + rows - size, size)], kvw.at[kind, block(off)],
            w_send, w_recv.at[off - 1], peer(off),
        )

    lane = lax.broadcasted_iota(jnp.int32, (1, cols), 1)
    row_id = lane
    for h in range(1, heads):
        row_id = row_id - jnp.where(lane >= h * rows, rows, 0)
    row_id = row_id + me * rows
    start = jnp.zeros((1, cols), jnp.int32)
    bound = jnp.int32(0)
    for j in range(len_ref.shape[0]):
        length = len_ref[j]
        bound = bound + length
        start = start + jnp.where(bound <= row_id, length, 0)

    wait_bytes(qs, load_sem.at[0])
    wait_bytes(dos, load_sem.at[1])

    stats = [None, None, None]

    def forward(index, keys, values, base, size, off=None):
        s = dot(keys, qs[...], 1, 1) * to_log2
        if off is not None:
            first = me * rows - (ahead if off == reach else off * rows)
            key_id = lax.broadcasted_iota(jnp.int32, (size, cols), 0) + first
            allowed = key_id >= start
            if off == 0:
                allowed = allowed & (key_id <= row_id)
            s = jnp.where(allowed, s, -jnp.inf)
        dp = dot(values, dos[...], 1, 1)
        high = jnp.max(s, axis=0, keepdims=True)
        if stats[0] is not None:
            high = jnp.maximum(high, stats[0])
        e = jnp.exp2(s - high)
        total = jnp.sum(e, axis=0, keepdims=True)
        weighted = jnp.sum(e * dp, axis=0, keepdims=True)
        if stats[0] is not None:
            shrink = jnp.exp2(stats[0] - high)
            total = total + stats[1] * shrink
            weighted = weighted + stats[2] * shrink
        stats[0], stats[1], stats[2] = high, total, weighted
        ebuf[base, :] = e
        dpbuf[base, :] = dp
        mbuf[index] = jnp.broadcast_to(high, (8, cols))

    w_index = GROUP + ny

    def e_block(off):
        rows_at = block(off)
        return pl.ds(total_p + rows_at.start, rows_at.size)

    def forward_window(off):
        wait_bytes(kvw.at[other, block(off)], wf_recv.at[off])
        forward(
            w_index + off, kvw[0, block(off)], kvw[1, block(off)], e_block(off),
            block(off).size, off,
        )

    def index_a(bz):
        return lax.rem(z + bz, GROUP)

    def index_b(by):
        return lax.rem(y + by, ny)

    def forward_a(bz):
        pz = index_a(bz)
        wait_bytes(kvp.at[other, part_a(pz)], pf_recv.at[pz])
        forward(pz, kvp[0, part_a(pz)], kvp[1, part_a(pz)], part_a(pz), size_a)

    def forward_b(by):
        py = index_b(by)
        wait_bytes(kvp.at[other, part_b(py)], pf_recv.at[GROUP + py])
        forward(GROUP + py, kvp[0, part_b(py)], kvp[1, part_b(py)], part_b(py), size_b)

    def pass_a(bz):
        pz = index_a(bz)
        mine = kvp.at[kind, part_a(pz)]
        if bz:
            wait_bytes(mine, a_recv.at[pz])
        copy_to(mine, mine, pf_send, pf_recv.at[pz], mate)

    def pass_b(by):
        py = index_b(by)
        mine = kvp.at[kind, part_b(py)]
        if by:
            wait_bytes(mine, b_recv.at[py])
        copy_to(mine, mine, pf_send, pf_recv.at[GROUP + py], mate)

    def pass_window(off):
        mine = kvw.at[kind, block(off)]
        wait_bytes(mine, w_recv.at[off - 1])
        copy_to(mine, mine, wf_send, wf_recv.at[off], mate)

    forward_window(0)
    mine_b = kvp.at[kind, part_b(y)]
    wait_bytes(mine_b, b_piece)
    for by in y_order:
        copy_to(mine_b, mine_b, two_send, b_recv.at[y], device(by, 0))
    mine_a = kvp.at[kind, part_a(z)]
    wait_bytes(mine_a, a_piece)
    for bz in z_order:
        copy_to(mine_a, mine_a, two_send, a_recv.at[z], device(0, bz))

    steps = [(pass_b, forward_b, 0), (pass_a, forward_a, 0)]
    steps += [(pass_window, forward_window, off) for off in (1, 4, 3, 2, 5, 6)[-reach:]]
    steps += [(pass_b, forward_b, by) for by in y_order[:2]]
    steps += [(pass_a, forward_a, bz) for bz in z_order[:2]]
    steps += [(pass_b, forward_b, by) for by in y_order[2:4]]
    steps += [(pass_a, forward_a, bz) for bz in z_order[2:]]
    steps += [(pass_b, forward_b, by) for by in y_order[4:]]
    for i in range(len(steps) + AHEAD):
        if i < len(steps):
            steps[i][0](steps[i][2])
        if i >= AHEAD:
            steps[i - AHEAD][1](steps[i - AHEAD][2])

    high, total, weighted = stats
    inverse = 1.0 / total
    delta = weighted * inverse

    def backward(index, base):
        factor = jnp.exp2(mbuf[index][:1] - high) * inverse
        w = ebuf[base, :] * factor
        wb = w.astype(BF16)
        ds = (w * (dpbuf[base, :] - delta)).astype(BF16)
        wbuf[base, :] = wb
        dsbuf[base, :] = ds
        return dot(ds, qs[...], 1, 0) * scale, dot(wb, dos[...], 1, 0)

    def backward_prompt(index, rows_at):
        dk, dv = backward(index, rows_at)
        gp[0, rows_at] = dk.astype(BF16)
        gp[1, rows_at] = dv.astype(BF16)
        copy_to(gp.at[other, rows_at], gpin.at[rows_at], gx_send, gx_recv.at[index], mate)

    def finish_prompt(index, rows_at, pieces, holds_own):
        wait_bytes(gpin.at[rows_at], gx_recv.at[index])
        gpout[rows_at, :] = (gp[kind, rows_at].astype(F32) + gpin[rows_at, :].astype(F32)).astype(BF16)
        for j, to in pieces:
            src = gpout.at[pl.ds(pl.multiple_of(rows_at.start + j * plocal, plocal), plocal)]
            if not holds_own:
                copy_to(src, rs.at[me], rs_send, rs_recv, {"resp": to})
                continue

            @pl.when(to != me)
            def _():
                copy_to(src, rs.at[me], rs_send, rs_recv, {"resp": to})

    def backward_a(bz):
        pz = index_a(bz)
        backward_prompt(pz, part_a(pz))

    def backward_b(by):
        py = index_b(by)
        backward_prompt(GROUP + py, part_b(py))

    def finish_a(bz):
        pz = index_a(bz)
        turn = [lax.rem(y // 2 + j, ny // 2) for j in range(ny // 2)]
        pieces = [(j, (2 * j + lax.rem(pz, 2)) * GROUP + pz) for j in turn]
        finish_prompt(pz, part_a(pz), pieces, bz == 0)

    def finish_b(by):
        py = index_b(by)
        pieces = [(j, py * GROUP + 2 * j + 1 - lax.rem(py, 2)) for j in range(GROUP // 2)]
        finish_prompt(GROUP + py, part_b(py), pieces, by == 0)

    def backward_window(off):
        dk, dv = backward(w_index + off, e_block(off))
        gw[0, block(off)] = dk.astype(BF16)
        gw[1, block(off)] = dv.astype(BF16)
        copy_to(gw.at[other, block(off)], gwin.at[block(off)], gwx_send, gwx_recv.at[off], mate)

    def finish_window(off):
        wait_bytes(gwin.at[block(off)], gwx_recv.at[off])
        both = gw[kind, block(off)].astype(F32) + gwin[block(off), :].astype(F32)
        if off == 0:
            return both
        gwout[block(off), :] = both.astype(BF16)
        size = block(off).size
        copy_to(
            gwout.at[block(off)], wr.at[off - 1, pl.ds(0, size)], wr_send, wr_recv.at[off - 1],
            peer(-off),
        )
        return None

    far_y = y_order[::-1]
    back = [(backward_a, finish_a, bz) for bz in (2, 1, 3)]
    back += [(backward_window, finish_window, off) for off in range(reach, reach - 3, -1)]
    back += [(backward_b, finish_b, by) for by in far_y[:4]]
    back += [(backward_window, finish_window, off) for off in range(reach - 3, 0, -1)]
    back += [(backward_b, finish_b, by) for by in far_y[4:]]
    back += [(backward_a, finish_a, 0), (backward_b, finish_b, 0)]
    back.append((backward_window, finish_window, 0))
    for i in range(len(back) + BEHIND):
        if i < len(back):
            back[i][0](back[i][2])
        if i >= BEHIND:
            own_grad = back[i - BEHIND][1](back[i - BEHIND][2])
    rs[me] = gpout[own_p, :]

    p_part = pl.ds(0, total_p)
    w_part = pl.ds(total_p, ahead + rows)
    out_t = dot(kvp[1], wbuf[p_part, :], 0, 0) + dot(kvw[1], wbuf[w_part, :], 0, 0)
    os[...] = out_t.T.astype(BF16)
    for h in range(heads):
        pltpu.make_async_copy(
            os.at[pl.ds(h * rows, rows)], att_hbm.at[:, pl.ds(h * d, d)], out_sem.at[0]
        ).start()
    dq_t = dot(kvp[0], dsbuf[p_part, :], 0, 0) + dot(kvw[0], dsbuf[w_part, :], 0, 0)
    dqs[...] = (dq_t.T * scale).astype(BF16)
    for h in range(heads):
        pltpu.make_async_copy(
            dqs.at[pl.ds(h * rows, rows)], dq_hbm.at[:, pl.ds(h * d, d)], out_sem.at[1]
        ).start()

    for off in range(1, reach):
        wait_bytes(wr.at[off - 1], wr_recv.at[off - 1])
        own_grad = own_grad + wr[off - 1].astype(F32)
    far = wr.at[reach - 1, pl.ds(0, tail)]
    wait_bytes(far, wr_recv.at[reach - 1])
    own_grad = jnp.concatenate(
        [own_grad[: rows - tail], own_grad[rows - tail :] + far[...].astype(F32)], axis=0
    )
    dkvs[...] = own_grad.astype(BF16)
    dkv_copy = pltpu.make_async_copy(dkvs, dkv_hbm, out_sem.at[2])
    dkv_copy.start()
    wait_bytes(rs.at[pl.ds(0, count - 1)], rs_recv)
    dpkvs[...] = jnp.sum(rs[...].astype(F32), axis=0).astype(BF16)
    dpkv_copy = pltpu.make_async_copy(dpkvs, dpkv_hbm, out_sem.at[3])
    dpkv_copy.start()

    @pl.when(odd == 0)
    def _():
        wait_bytes(kvp.at[0, pl.ds(0, (ny - 1) * plocal)], one_send.at[0])

    @pl.when(odd == 1)
    def _():
        wait_bytes(kvp.at[0, pl.ds(0, (GROUP - 1) * plocal)], one_send.at[1])

    wait_bytes(kvp.at[0, pl.ds(0, (GROUP - 1) * size_a + (ny - 1) * size_b)], two_send)
    wait_bytes(kvp.at[0], pf_send)
    wait_bytes(kvw.at[0, pl.ds(0, ahead)], w_send)
    wait_bytes(kvw.at[0], wf_send)
    wait_bytes(gpin, gx_send)
    wait_bytes(gwin, gwx_send)
    wait_bytes(rs.at[pl.ds(0, count - 1)], rs_send)
    wait_bytes(gwout.at[pl.ds(0, ahead)], wr_send)
    wait_bytes(os, out_sem.at[0])
    wait_bytes(dqs, out_sem.at[1])
    dkv_copy.wait()
    dpkv_copy.wait()


def shards(queries, response_key_value, prompt_key_value, output_cotangent, lengths):
    rows, width = queries.shape
    d = response_key_value.shape[1]
    cols = width // d * rows
    plocal = prompt_key_value.shape[0]
    count = lax.axis_size("resp")
    total_p = plocal * count
    ny = count // GROUP
    reach, tail = window_shape(rows)
    window = tail + reach * rows
    keys = total_p + window
    dma, anywhere = pltpu.SemaphoreType.DMA, pl.BlockSpec(memory_space=pl.ANY)
    whole = pl.BlockSpec(memory_space=pltpu.VMEM)
    limit = 60 * 1024 * 1024
    out_shape = (
        jax.ShapeDtypeStruct(queries.shape, BF16),
        jax.ShapeDtypeStruct(queries.shape, BF16),
        jax.ShapeDtypeStruct(response_key_value.shape, BF16),
        jax.ShapeDtypeStruct(prompt_key_value.shape, BF16),
    )
    results = pl.pallas_call(
        functools.partial(kernel, count),
        out_shape=out_shape,
        in_specs=[anywhere] * 4 + [pl.BlockSpec(memory_space=pltpu.SMEM)],
        out_specs=(anywhere,) * 4,
        scratch_shapes=[
            pltpu.VMEM((cols, d), BF16),
            pltpu.VMEM((cols, d), BF16),
            pltpu.VMEM((2, total_p, d), BF16),
            pltpu.VMEM((2, window, d), BF16),
            pltpu.VMEM((keys, cols), F32),
            pltpu.VMEM((keys, cols), F32),
            pltpu.VMEM((GROUP + ny + reach + 1, 8, cols), F32),
            pltpu.VMEM((keys, cols), BF16),
            pltpu.VMEM((keys, cols), BF16),
            pltpu.VMEM((2, total_p, d), BF16),
            pltpu.VMEM((total_p, d), BF16),
            pltpu.VMEM((total_p, d), BF16),
            pltpu.VMEM((count, plocal, d), BF16),
            pltpu.VMEM((2, window, d), BF16),
            pltpu.VMEM((window, d), BF16),
            pltpu.VMEM((window, d), BF16),
            pltpu.VMEM((reach, rows, d), BF16),
            pltpu.VMEM((cols, d), BF16),
            pltpu.VMEM((cols, d), BF16),
            pltpu.VMEM((rows, d), BF16),
            pltpu.VMEM((plocal, d), BF16),
            dma((2,)), dma, dma((2,)), dma, dma, dma, dma((GROUP,)), dma((ny,)),
            dma, dma((GROUP + ny,)),
            dma, dma((reach,)), dma, dma((reach + 1,)),
            dma, dma((GROUP + ny,)), dma, dma((reach + 1,)),
            dma, dma, dma, dma((reach,)),
            dma((4,)),
        ],
        compiler_params=pltpu.CompilerParams(
            collective_id=0, has_side_effects=True, vmem_limit_bytes=limit
        ),
    )(queries, response_key_value, prompt_key_value, output_cotangent, lengths)
    return pl.pallas_call(
        copy_kernel,
        out_shape=out_shape,
        in_specs=[whole] * 4,
        out_specs=(whole,) * 4,
        compiler_params=pltpu.CompilerParams(vmem_limit_bytes=limit),
    )(*results)


def solution(mesh):
    spec = P("resp", "head")
    return jax.shard_map(
        shards,
        mesh=mesh,
        in_specs=(spec, spec, spec, spec, P()),
        out_specs=(spec, spec, spec, spec),
        check_vma=False,
    )
```

```python
import functools
import math

import jax
import jax.numpy as jnp
from jax import lax
from jax.experimental import pallas as pl
from jax.experimental.pallas import tpu as pltpu
from jax.sharding import PartitionSpec as P

MAXLEN = 512
GROUP = 4
AHEAD = 2
BEHIND = 3
MESH = pl.DeviceIdType.MESH
F32 = jnp.float32
BF16 = jnp.bfloat16


def dot(a, b, ca, cb):
    return lax.dot_general(a, b, (((ca,), (cb,)), ((), ())), preferred_element_type=F32)


def wait_bytes(ref, sem):
    pltpu.make_async_copy(ref, ref, sem).wait()


def copy_to(src, dst, send, recv, to):
    pltpu.make_async_remote_copy(
        src_ref=src, dst_ref=dst, send_sem=send, recv_sem=recv, device_id=to, device_id_type=MESH
    ).start()


def at(index, size):
    return pl.ds(pl.multiple_of(index * size, size), size)


def copy_kernel(*refs):
    half = len(refs) // 2
    for i in range(half):
        refs[half + i][...] = refs[i][...]


def window_shape(rows):
    reach = (MAXLEN + rows - 2) // rows
    return reach, -(-(MAXLEN - 1 - (reach - 1) * rows) // 16) * 16


def kernel(
    count,
    q_hbm, kv_hbm, pkv_hbm, do_hbm, len_ref,
    att_ref, dq_ref, dkv_ref, dpkv_ref,
    qs, dos, kvp, kvw, ebuf, dpbuf, mbuf, wbuf, dsbuf,
    gp, gpin, gpout, rs, gw, gwin, gwout, wr,
    load_sem, kv_sem, one_send, a_piece, b_piece, two_send, a_recv, b_recv, pf_send, pf_recv,
    w_send, w_recv, wf_send, wf_recv,
    gx_send, gx_recv, gwx_send, gwx_recv, rs_send, rs_recv, wr_send, wr_recv,
):
    rows, width = q_hbm.shape
    d = kv_hbm.shape[1]
    heads = width // d
    cols = heads * rows
    plocal = pkv_hbm.shape[0]
    ny = count // GROUP
    size_a = ny // 2 * plocal
    size_b = GROUP // 2 * plocal
    reach, tail = window_shape(rows)
    ahead = tail + (reach - 1) * rows
    scale = 1.0 / math.sqrt(d)
    to_log2 = scale * math.log2(math.e)

    me = lax.axis_index("resp")
    head = lax.axis_index("head")
    kind = lax.rem(head, 2)
    other = 1 - kind
    mate = {"head": head + 1 - 2 * kind}
    y, z = me // GROUP, lax.rem(me, GROUP)

    def device(by, bz):
        return {"resp": lax.rem(y + by, ny) * GROUP + lax.rem(z + bz, GROUP)}

    def peer(by):
        return {"resp": lax.rem(me + by + count, count)}

    odd = lax.rem(y + z, 2)
    own_index = (1 - odd) * (z * (ny // 2) + y // 2) + odd * (
        GROUP * (ny // 2) + y * (GROUP // 2) + z // 2
    )
    own_p = at(own_index, plocal)

    def part_a(pz):
        return at(pz, size_a)

    def part_b(py):
        return pl.ds(pl.multiple_of(GROUP * size_a + py * size_b, size_b), size_b)

    def block(off):
        if off == reach:
            return pl.ds(0, tail)
        return pl.ds(tail + (reach - 1 - off) * rows, rows)

    own_w = block(0)
    z_order = (1, 3, 2)
    y_order = sorted(range(1, ny), key=lambda by: min(by, ny - by))

    kv_copy = pltpu.make_async_copy(kv_hbm, kvw.at[kind, own_w], kv_sem)
    kv_copy.start()

    own_copy = pltpu.make_async_copy(pkv_hbm, kvp.at[kind, own_p], load_sem.at[2])
    own_copy.start()
    for h in range(heads):
        pltpu.make_async_copy(
            q_hbm.at[:, pl.ds(h * d, d)], qs.at[pl.ds(h * rows, rows)], load_sem.at[0]
        ).start()
        pltpu.make_async_copy(
            do_hbm.at[:, pl.ds(h * d, d)], dos.at[pl.ds(h * rows, rows)], load_sem.at[1]
        ).start()

    barrier = pltpu.get_barrier_semaphore()
    greeted = [device(by, 0) for by in y_order] + [device(0, bz) for bz in z_order]
    greeted += [peer(by) for off in range(1, reach + 1) if off % GROUP for by in (off, -off)]
    pl.semaphore_signal(barrier, inc=1, device_id=mate, device_id_type=MESH)
    for to in greeted:
        pl.semaphore_signal(barrier, inc=1, device_id=to, device_id_type=MESH)
    pl.semaphore_wait(barrier, len(greeted) + 1)

    def send_along_y(rows_at, send, arrived):
        for by in y_order:
            copy_to(kvp.at[kind, rows_at], kvp.at[kind, rows_at], send, arrived, device(by, 0))

    def send_along_z(rows_at, send, arrived):
        for bz in z_order:
            copy_to(kvp.at[kind, rows_at], kvp.at[kind, rows_at], send, arrived, device(0, bz))

    own_copy.wait()

    @pl.when(odd == 0)
    def _():
        send_along_y(own_p, one_send.at[0], a_piece.at[y // 2])
        send_along_z(own_p, two_send, a_recv.at[z])

    @pl.when(odd == 1)
    def _():
        send_along_z(own_p, one_send.at[1], b_piece.at[z // 2])
        send_along_y(own_p, two_send, b_recv.at[y])

    kv_copy.wait()
    copy_to(kvw.at[kind, own_w], kvw.at[kind, own_w], wf_send, wf_recv.at[0], mate)
    for off in range(1, reach + 1):
        size = tail if off == reach else rows
        copy_to(
            kvw.at[kind, pl.ds(ahead + rows - size, size)], kvw.at[kind, block(off)],
            w_send, w_recv.at[off - 1], peer(off),
        )

    lane = lax.broadcasted_iota(jnp.int32, (1, cols), 1)
    row_id = lane
    for h in range(1, heads):
        row_id = row_id - jnp.where(lane >= h * rows, rows, 0)
    row_id = row_id + me * rows
    start = jnp.zeros((1, cols), jnp.int32)
    bound = jnp.int32(0)
    for j in range(len_ref.shape[0]):
        length = len_ref[j]
        bound = bound + length
        start = start + jnp.where(bound <= row_id, length, 0)

    wait_bytes(qs, load_sem.at[0])
    wait_bytes(dos, load_sem.at[1])

    stats = [None, None, None]

    def forward(index, sources, off=None):
        keys = jnp.concatenate([buffer[0, at_rows] for buffer, at_rows, _, _ in sources], axis=0)
        values = jnp.concatenate([buffer[1, at_rows] for buffer, at_rows, _, _ in sources], axis=0)
        s = dot(keys, qs[...], 1, 1) * to_log2
        dp = dot(values, dos[...], 1, 1)
        if sources[0][3] is not None:
            masks = []
            for _, at_rows, _, off in sources:
                first = me * rows - (ahead if off == reach else off * rows)
                key_id = lax.broadcasted_iota(jnp.int32, (at_rows.size, cols), 0) + first
                masks.append((key_id >= start) & (key_id <= row_id))
            s = jnp.where(jnp.concatenate(masks, axis=0), s, -jnp.inf)
        high = jnp.max(s, axis=0, keepdims=True)
        if stats[0] is not None:
            high = jnp.maximum(high, stats[0])
        e = jnp.exp2(s - high)
        total = jnp.sum(e, axis=0, keepdims=True)
        weighted = jnp.sum(e * dp, axis=0, keepdims=True)
        if stats[0] is not None:
            shrink = jnp.exp2(stats[0] - high)
            total = total + stats[1] * shrink
            weighted = weighted + stats[2] * shrink
        stats[0], stats[1], stats[2] = high, total, weighted
        done = 0
        for _, _, base, _ in sources:
            ebuf[base, :] = e[done : done + base.size]
            dpbuf[base, :] = dp[done : done + base.size]
            done += base.size
        mbuf[index] = jnp.broadcast_to(high, (8, cols))

    total_p = count * plocal

    def e_block(off):
        rows_at = block(off)
        return pl.ds(total_p + rows_at.start, rows_at.size)

    def index_a(bz):
        return lax.rem(z + bz, GROUP)

    def index_b(by):
        return lax.rem(y + by, ny)

    def source(item):
        what, n = item
        if what == "a":
            return kvp, part_a(index_a(n)), part_a(index_a(n)), None
        if what == "b":
            return kvp, part_b(index_b(n)), part_b(index_b(n)), None
        return kvw, block(n), e_block(n), n

    def passed(item):
        what, n = item
        if what == "a":
            return pf_recv.at[index_a(n)]
        if what == "b":
            return pf_recv.at[GROUP + index_b(n)]
        return wf_recv.at[n]

    def forward_group(index):
        for item in groups[index]:
            buffer, at_rows, _, _ = source(item)
            wait_bytes(buffer.at[other, at_rows], passed(item))
        forward(index, [source(item) for item in groups[index]])

    def pass_a(bz):
        pz = index_a(bz)
        mine = kvp.at[kind, part_a(pz)]
        if bz:
            wait_bytes(mine, a_recv.at[pz])
        copy_to(mine, mine, pf_send, pf_recv.at[pz], mate)

    def pass_b(by):
        py = index_b(by)
        mine = kvp.at[kind, part_b(py)]
        if by:
            wait_bytes(mine, b_recv.at[py])
        copy_to(mine, mine, pf_send, pf_recv.at[GROUP + py], mate)

    def pass_window(off):
        mine = kvw.at[kind, block(off)]
        wait_bytes(mine, w_recv.at[off - 1])
        copy_to(mine, mine, wf_send, wf_recv.at[off], mate)

    passes = {"a": pass_a, "b": pass_b, "w": pass_window}
    groups = [[("w", 0)], [("b", 0), ("a", 0)]]
    groups += [[("w", off) for off in offs] for offs in ((1, 4), (3, 2), (5, 6))]
    pairs = [[("b", by) for by in y_order[i : i + 2]] for i in range(0, max(len(y_order) - 1, 1), 2)]
    if len(y_order) > 1:
        pairs[-1].append(("b", y_order[-1]))
    groups += pairs[:1] + [[("a", bz)] for bz in z_order[:2]] + pairs[1:2]
    groups += [[("a", bz)] for bz in z_order[2:]] + pairs[2:]

    forward_group(0)
    def pass_on_a(by):
        place = lax.rem(y + by, ny) // 2
        rows_at = at(z * (ny // 2) + place, plocal)
        wait_bytes(kvp.at[kind, rows_at], a_piece.at[place])
        send_along_z(rows_at, two_send, a_recv.at[z])

    def pass_on_b(bz):
        place = lax.rem(z + bz, GROUP) // 2
        rows_at = at(GROUP * (ny // 2) + y * (GROUP // 2) + place, plocal)
        wait_bytes(kvp.at[kind, rows_at], b_piece.at[place])
        send_along_y(rows_at, two_send, b_recv.at[y])

    @pl.when(odd == 0)
    def _():
        for bz in (1, 3):
            pass_on_b(bz)
        for by in y_order:
            if by % 2 == 0:
                pass_on_a(by)

    @pl.when(odd == 1)
    def _():
        for by in y_order:
            if by % 2 == 1:
                pass_on_a(by)
        pass_on_b(2)

    for i in range(1, len(groups) + AHEAD):
        if i < len(groups):
            for what, n in groups[i]:
                passes[what](n)
        if i > AHEAD:
            forward_group(i - AHEAD)

    high, total, weighted = stats
    inverse = 1.0 / total
    delta = weighted * inverse

    def backward(index):
        sources = [source(item) for item in groups[index]]
        factor = jnp.exp2(mbuf[index][:1] - high) * inverse
        w = jnp.concatenate([ebuf[base, :] for _, _, base, _ in sources], axis=0) * factor
        dp = jnp.concatenate([dpbuf[base, :] for _, _, base, _ in sources], axis=0)
        wb = w.astype(BF16)
        ds = (w * (dp - delta)).astype(BF16)
        dk = (dot(ds, qs[...], 1, 0) * scale).astype(BF16)
        dv = dot(wb, dos[...], 1, 0).astype(BF16)
        done = 0
        for item, (buffer, at_rows, base, _) in zip(groups[index], sources):
            now = slice(done, done + base.size)
            done += base.size
            wbuf[base, :] = wb[now]
            dsbuf[base, :] = ds[now]
            own, received, send, arrived = grads(item)
            own[0, at_rows] = dk[now]
            own[1, at_rows] = dv[now]
            copy_to(own.at[other, at_rows], received.at[at_rows], send, arrived, mate)

    def grads(item):
        what, n = item
        if what == "w":
            return gw, gwin, gwx_send, gwx_recv.at[n]
        return gp, gpin, gx_send, gx_recv.at[index_a(n) if what == "a" else GROUP + index_b(n)]

    def finish_prompt(index, rows_at, pieces, holds_own):
        wait_bytes(gpin.at[rows_at], gx_recv.at[index])
        gpout[rows_at, :] = (gp[kind, rows_at].astype(F32) + gpin[rows_at, :].astype(F32)).astype(BF16)
        for j, to in pieces:
            src = gpout.at[pl.ds(pl.multiple_of(rows_at.start + j * plocal, plocal), plocal)]
            if not holds_own:
                copy_to(src, rs.at[me], rs_send, rs_recv, {"resp": to})
                continue

            @pl.when(to != me)
            def _():
                copy_to(src, rs.at[me], rs_send, rs_recv, {"resp": to})

    def finish_a(bz):
        pz = index_a(bz)
        turn = [lax.rem(y // 2 + j, ny // 2) for j in range(ny // 2)]
        pieces = [(j, (2 * j + lax.rem(pz, 2)) * GROUP + pz) for j in turn]
        finish_prompt(pz, part_a(pz), pieces, bz == 0)

    def finish_b(by):
        py = index_b(by)
        pieces = [(j, py * GROUP + 2 * j + 1 - lax.rem(py, 2)) for j in range(GROUP // 2)]
        finish_prompt(GROUP + py, part_b(py), pieces, by == 0)

    def finish_window(off):
        wait_bytes(gwin.at[block(off)], gwx_recv.at[off])
        both = gw[kind, block(off)].astype(F32) + gwin[block(off), :].astype(F32)
        if off == 0:
            return both
        gwout[block(off), :] = both.astype(BF16)
        size = block(off).size
        copy_to(
            gwout.at[block(off)], wr.at[off - 1, pl.ds(0, size)], wr_send, wr_recv.at[off - 1],
            peer(-off),
        )
        return None

    finishes = {"a": finish_a, "b": finish_b, "w": finish_window}
    back = list(range(len(groups) - 1, -1, -1))
    for i in range(len(back) + BEHIND):
        if i < len(back):
            backward(back[i])
        if i >= BEHIND:
            for what, n in groups[back[i - BEHIND]]:
                own_grad = finishes[what](n)
    rs[me] = gpout[own_p, :]

    p_part = pl.ds(0, total_p)
    w_part = pl.ds(total_p, ahead + rows)
    out_t = dot(kvp[1], wbuf[p_part, :], 0, 0) + dot(kvw[1], wbuf[w_part, :], 0, 0)
    out = out_t.T.astype(BF16)
    for h in range(heads):
        att_ref[:, h * d : (h + 1) * d] = out[h * rows : (h + 1) * rows]
    dq_t = dot(kvp[0], dsbuf[p_part, :], 0, 0) + dot(kvw[0], dsbuf[w_part, :], 0, 0)
    dq = (dq_t.T * scale).astype(BF16)
    for h in range(heads):
        dq_ref[:, h * d : (h + 1) * d] = dq[h * rows : (h + 1) * rows]

    for off in range(1, reach):
        wait_bytes(wr.at[off - 1], wr_recv.at[off - 1])
        own_grad = own_grad + wr[off - 1].astype(F32)
    far = wr.at[reach - 1, pl.ds(0, tail)]
    wait_bytes(far, wr_recv.at[reach - 1])
    own_grad = jnp.concatenate(
        [own_grad[: rows - tail], own_grad[rows - tail :] + far[...].astype(F32)], axis=0
    )
    dkv_ref[...] = own_grad.astype(BF16)
    wait_bytes(rs.at[pl.ds(0, count - 1)], rs_recv)
    dpkv_ref[...] = jnp.sum(rs[...].astype(F32), axis=0).astype(BF16)

    @pl.when(odd == 0)
    def _():
        wait_bytes(kvp.at[0, pl.ds(0, (ny - 1) * plocal)], one_send.at[0])

    @pl.when(odd == 1)
    def _():
        wait_bytes(kvp.at[0, pl.ds(0, (GROUP - 1) * plocal)], one_send.at[1])

    wait_bytes(kvp.at[0, pl.ds(0, (GROUP - 1) * size_a + (ny - 1) * size_b)], two_send)
    wait_bytes(kvp.at[0], pf_send)
    wait_bytes(kvw.at[0, pl.ds(0, ahead)], w_send)
    wait_bytes(kvw.at[0], wf_send)
    wait_bytes(gpin, gx_send)
    wait_bytes(gwin, gwx_send)
    wait_bytes(rs.at[pl.ds(0, count - 1)], rs_send)
    wait_bytes(gwout.at[pl.ds(0, ahead)], wr_send)


def shards(queries, response_key_value, prompt_key_value, output_cotangent, lengths):
    rows, width = queries.shape
    d = response_key_value.shape[1]
    cols = width // d * rows
    plocal = prompt_key_value.shape[0]
    count = lax.axis_size("resp")
    total_p = plocal * count
    ny = count // GROUP
    reach, tail = window_shape(rows)
    window = tail + reach * rows
    keys = total_p + window
    dma, anywhere = pltpu.SemaphoreType.DMA, pl.BlockSpec(memory_space=pl.ANY)
    whole = pl.BlockSpec(memory_space=pltpu.VMEM)
    limit = 60 * 1024 * 1024
    out_shape = (
        jax.ShapeDtypeStruct(queries.shape, BF16),
        jax.ShapeDtypeStruct(queries.shape, BF16),
        jax.ShapeDtypeStruct(response_key_value.shape, BF16),
        jax.ShapeDtypeStruct(prompt_key_value.shape, BF16),
    )
    results = pl.pallas_call(
        functools.partial(kernel, count),
        out_shape=tuple(pltpu.VMEM(s.shape, s.dtype) for s in out_shape),
        in_specs=[anywhere] * 4 + [pl.BlockSpec(memory_space=pltpu.SMEM)],
        out_specs=(whole,) * 4,
        scratch_shapes=[
            pltpu.VMEM((cols, d), BF16),
            pltpu.VMEM((cols, d), BF16),
            pltpu.VMEM((2, total_p, d), BF16),
            pltpu.VMEM((2, window, d), BF16),
            pltpu.VMEM((keys, cols), F32),
            pltpu.VMEM((keys, cols), F32),
            pltpu.VMEM((GROUP + ny + reach + 1, 8, cols), F32),
            pltpu.VMEM((keys, cols), BF16),
            pltpu.VMEM((keys, cols), BF16),
            pltpu.VMEM((2, total_p, d), BF16),
            pltpu.VMEM((total_p, d), BF16),
            pltpu.VMEM((total_p, d), BF16),
            pltpu.VMEM((count, plocal, d), BF16),
            pltpu.VMEM((2, window, d), BF16),
            pltpu.VMEM((window, d), BF16),
            pltpu.VMEM((window, d), BF16),
            pltpu.VMEM((reach, rows, d), BF16),
            dma((3,)), dma, dma((2,)), dma((ny // 2,)), dma((GROUP // 2,)), dma, dma((GROUP,)),
            dma((ny,)),
            dma, dma((GROUP + ny,)),
            dma, dma((reach,)), dma, dma((reach + 1,)),
            dma, dma((GROUP + ny,)), dma, dma((reach + 1,)),
            dma, dma, dma, dma((reach,)),
        ],
        compiler_params=pltpu.CompilerParams(
            collective_id=0, has_side_effects=True, vmem_limit_bytes=limit
        ),
    )(queries, response_key_value, prompt_key_value, output_cotangent, lengths)
    return pl.pallas_call(
        copy_kernel,
        out_shape=out_shape,
        in_specs=[whole] * 4,
        out_specs=(whole,) * 4,
        compiler_params=pltpu.CompilerParams(vmem_limit_bytes=limit),
    )(*[pltpu.with_memory_space_constraint(r, pltpu.VMEM) for r in results])


def solution(mesh):
    spec = P("resp", "head")
    return jax.shard_map(
        shards,
        mesh=mesh,
        in_specs=(spec, spec, spec, spec, P()),
        out_specs=(spec, spec, spec, spec),
        check_vma=False,
    )
```

```python
import functools
import math

import jax
import jax.numpy as jnp
from jax import lax
from jax.experimental import pallas as pl
from jax.experimental.pallas import tpu as pltpu
from jax.sharding import PartitionSpec as P

MAXLEN = 512
GROUP = 4
AHEAD = 2
BEHIND = 3
MESH = pl.DeviceIdType.MESH
F32 = jnp.float32
BF16 = jnp.bfloat16


def dot(a, b, ca, cb):
    return lax.dot_general(a, b, (((ca,), (cb,)), ((), ())), preferred_element_type=F32)


def wait_bytes(ref, sem):
    pltpu.make_async_copy(ref, ref, sem).wait()


def copy_to(src, dst, send, recv, to):
    pltpu.make_async_remote_copy(
        src_ref=src, dst_ref=dst, send_sem=send, recv_sem=recv, device_id=to, device_id_type=MESH
    ).start()


def at(index, size):
    return pl.ds(pl.multiple_of(index * size, size), size)


def copy_kernel(*refs):
    half = len(refs) // 2
    for i in range(half):
        refs[half + i][...] = refs[i][...]


def window_shape(rows):
    reach = (MAXLEN + rows - 2) // rows
    return reach, -(-(MAXLEN - 1 - (reach - 1) * rows) // 16) * 16


def kernel(
    count,
    q_hbm, kv_hbm, pkv_hbm, do_hbm, len_ref,
    att_ref, dq_ref, dkv_ref, dpkv_ref,
    qs, dos, kvp, kvw, ebuf, dpbuf, mbuf, wbuf, dsbuf,
    gp, gpin, gpout, rs, gw, gwin, gwout, wr,
    load_sem, kv_sem, one_send, a_piece, b_piece, two_send, a_recv, b_recv, pf_send, pf_recv,
    w_send, w_recv, wf_send, wf_recv,
    gx_send, gx_recv, gwx_send, gwx_recv, rs_send, rs_recv, wr_send, wr_recv,
):
    rows, width = q_hbm.shape
    d = kv_hbm.shape[1]
    heads = width // d
    cols = heads * rows
    plocal = pkv_hbm.shape[0]
    ny = count // GROUP
    size_a = ny // 2 * plocal
    size_b = GROUP // 2 * plocal
    reach, tail = window_shape(rows)
    ahead = tail + (reach - 1) * rows
    scale = 1.0 / math.sqrt(d)
    to_log2 = scale * math.log2(math.e)

    me = lax.axis_index("resp")
    head = lax.axis_index("head")
    kind = lax.rem(head, 2)
    other = 1 - kind
    mate = {"head": head + 1 - 2 * kind}
    y, z = me // GROUP, lax.rem(me, GROUP)

    def device(by, bz):
        return {"resp": lax.rem(y + by, ny) * GROUP + lax.rem(z + bz, GROUP)}

    def peer(by):
        return {"resp": lax.rem(me + by + count, count)}

    odd = lax.rem(y + z, 2)
    own_index = (1 - odd) * (z * (ny // 2) + y // 2) + odd * (
        GROUP * (ny // 2) + y * (GROUP // 2) + z // 2
    )
    own_p = at(own_index, plocal)

    def part_a(pz):
        return at(pz, size_a)

    def part_b(py):
        return pl.ds(pl.multiple_of(GROUP * size_a + py * size_b, size_b), size_b)

    def block(off):
        if not isinstance(off, int):
            return pl.ds(pl.multiple_of(tail + (reach - 1 - off) * rows, math.gcd(tail, rows)), rows)
        if off == reach:
            return pl.ds(0, tail)
        return pl.ds(tail + (reach - 1 - off) * rows, rows)

    own_w = block(0)
    z_order = (1, 3, 2)
    y_order = sorted(range(1, ny), key=lambda by: min(by, ny - by))

    kv_copy = pltpu.make_async_copy(kv_hbm, kvw.at[kind, own_w], kv_sem)
    kv_copy.start()

    own_copy = pltpu.make_async_copy(pkv_hbm, kvp.at[kind, own_p], load_sem.at[2])
    own_copy.start()
    for h in range(heads):
        pltpu.make_async_copy(
            q_hbm.at[:, pl.ds(h * d, d)], qs.at[pl.ds(h * rows, rows)], load_sem.at[0]
        ).start()
        pltpu.make_async_copy(
            do_hbm.at[:, pl.ds(h * d, d)], dos.at[pl.ds(h * rows, rows)], load_sem.at[1]
        ).start()

    barrier = pltpu.get_barrier_semaphore()
    greeted = [device(by, 0) for by in y_order] + [device(0, bz) for bz in z_order]
    greeted += [peer(by) for off in range(1, reach + 1) if off % GROUP for by in (off, -off)]
    pl.semaphore_signal(barrier, inc=1, device_id=mate, device_id_type=MESH)
    for to in greeted:
        pl.semaphore_signal(barrier, inc=1, device_id=to, device_id_type=MESH)
    pl.semaphore_wait(barrier, len(greeted) + 1)

    def send_along_y(rows_at, send, arrived):
        for by in y_order:
            copy_to(kvp.at[kind, rows_at], kvp.at[kind, rows_at], send, arrived, device(by, 0))

    def send_along_z(rows_at, send, arrived):
        for bz in z_order:
            copy_to(kvp.at[kind, rows_at], kvp.at[kind, rows_at], send, arrived, device(0, bz))

    own_copy.wait()

    @pl.when(odd == 0)
    def _():
        send_along_y(own_p, one_send.at[0], a_piece.at[y // 2])
        send_along_z(own_p, two_send, a_recv.at[z])

    @pl.when(odd == 1)
    def _():
        send_along_z(own_p, one_send.at[1], b_piece.at[z // 2])
        send_along_y(own_p, two_send, b_recv.at[y])

    kv_copy.wait()
    copy_to(kvw.at[kind, own_w], kvw.at[kind, own_w], wf_send, wf_recv.at[0], mate)
    for off in range(1, reach + 1):
        size = tail if off == reach else rows
        copy_to(
            kvw.at[kind, pl.ds(ahead + rows - size, size)], kvw.at[kind, block(off)],
            w_send, w_recv.at[off - 1], peer(off),
        )

    lane = lax.broadcasted_iota(jnp.int32, (1, cols), 1)
    row_id = lane
    for h in range(1, heads):
        row_id = row_id - jnp.where(lane >= h * rows, rows, 0)
    row_id = row_id + me * rows
    start = jnp.zeros((1, cols), jnp.int32)
    bound = jnp.int32(0)
    for j in range(len_ref.shape[0]):
        length = len_ref[j]
        bound = bound + length
        start = start + jnp.where(bound <= row_id, length, 0)

    wait_bytes(qs, load_sem.at[0])
    wait_bytes(dos, load_sem.at[1])

    stats = [None, None, None]

    def forward(slots, sources):
        keys = jnp.concatenate([buffer[0, at_rows] for buffer, at_rows, _, _ in sources], axis=0)
        values = jnp.concatenate([buffer[1, at_rows] for buffer, at_rows, _, _ in sources], axis=0)
        s = dot(keys, qs[...], 1, 1) * to_log2
        dp = dot(values, dos[...], 1, 1)
        if sources[0][3] is not None:
            masks = []
            for _, at_rows, _, off in sources:
                first = me * rows - (ahead if off == reach else off * rows)
                key_id = lax.broadcasted_iota(jnp.int32, (at_rows.size, cols), 0) + first
                masks.append((key_id >= start) & (key_id <= row_id))
            s = jnp.where(jnp.concatenate(masks, axis=0), s, -jnp.inf)
        high = jnp.max(s, axis=0, keepdims=True)
        if stats[0] is not None:
            high = jnp.maximum(high, stats[0])
        e = jnp.exp2(s - high)
        total = jnp.sum(e, axis=0, keepdims=True)
        weighted = jnp.sum(e * dp, axis=0, keepdims=True)
        if stats[0] is not None:
            shrink = jnp.exp2(stats[0] - high)
            total = total + stats[1] * shrink
            weighted = weighted + stats[2] * shrink
        stats[0], stats[1], stats[2] = high, total, weighted
        done = 0
        for slot, (_, _, base, _) in zip(slots, sources):
            mbuf[slot] = jnp.broadcast_to(high, (8, cols))
            ebuf[base, :] = e[done : done + base.size]
            dpbuf[base, :] = dp[done : done + base.size]
            done += base.size

    total_p = count * plocal

    def e_block(off):
        rows_at = block(off)
        if isinstance(off, int):
            return pl.ds(total_p + rows_at.start, rows_at.size)
        return pl.ds(pl.multiple_of(total_p + rows_at.start, math.gcd(tail, rows)), rows)

    def index_a(bz):
        return lax.rem(z + bz, GROUP)

    def index_b(by):
        return lax.rem(y + by, ny)

    def source(item):
        what, n = item
        if what == "a":
            return kvp, part_a(index_a(n)), part_a(index_a(n)), None
        if what == "b":
            return kvp, part_b(index_b(n)), part_b(index_b(n)), None
        return kvw, block(n), e_block(n), n

    def slot(item):
        what, n = item
        if what == "a":
            return index_a(n)
        return GROUP + index_b(n) if what == "b" else GROUP + ny + n

    def passed(item):
        what, n = item
        if what == "a":
            return pf_recv.at[index_a(n)]
        if what == "b":
            return pf_recv.at[GROUP + index_b(n)]
        return wf_recv.at[n]

    def forward_group(index):
        for item in groups[index]:
            buffer, at_rows, _, _ = source(item)
            wait_bytes(buffer.at[other, at_rows], passed(item))
        forward([slot(item) for item in groups[index]], [source(item) for item in groups[index]])

    def pass_a(bz):
        pz = index_a(bz)
        mine = kvp.at[kind, part_a(pz)]
        if bz:
            wait_bytes(mine, a_recv.at[pz])
        copy_to(mine, mine, pf_send, pf_recv.at[pz], mate)

    def pass_b(by):
        py = index_b(by)
        mine = kvp.at[kind, part_b(py)]
        if by:
            wait_bytes(mine, b_recv.at[py])
        copy_to(mine, mine, pf_send, pf_recv.at[GROUP + py], mate)

    def pass_window(off):
        mine = kvw.at[kind, block(off)]
        wait_bytes(mine, w_recv.at[off - 1])
        copy_to(mine, mine, wf_send, wf_recv.at[off], mate)

    passes = {"a": pass_a, "b": pass_b, "w": pass_window}
    groups = [[("w", 0)], [("b", 0), ("a", 0)]]
    groups += [[("w", off) for off in offs] for offs in ((1, 4), (3, 2), (5, 6))]
    pairs = [[("b", by) for by in y_order[i : i + 2]] for i in range(0, max(len(y_order) - 1, 1), 2)]
    if len(y_order) > 1:
        pairs[-1].append(("b", y_order[-1]))
    groups += pairs[:1] + [[("a", bz)] for bz in z_order[:2]] + pairs[1:2]
    groups += [[("a", bz)] for bz in z_order[2:]] + pairs[2:]

    forward_group(0)
    def pass_on_a(by):
        place = lax.rem(y + by, ny) // 2
        rows_at = at(z * (ny // 2) + place, plocal)
        wait_bytes(kvp.at[kind, rows_at], a_piece.at[place])
        send_along_z(rows_at, two_send, a_recv.at[z])

    def pass_on_b(bz):
        place = lax.rem(z + bz, GROUP) // 2
        rows_at = at(GROUP * (ny // 2) + y * (GROUP // 2) + place, plocal)
        wait_bytes(kvp.at[kind, rows_at], b_piece.at[place])
        send_along_y(rows_at, two_send, b_recv.at[y])

    @pl.when(odd == 0)
    def _():
        for bz in (1, 3):
            pass_on_b(bz)
        for by in y_order:
            if by % 2 == 0:
                pass_on_a(by)

    @pl.when(odd == 1)
    def _():
        for by in y_order:
            if by % 2 == 1:
                pass_on_a(by)
        pass_on_b(2)

    for i in range(1, len(groups) + AHEAD):
        if i < len(groups):
            for what, n in groups[i]:
                passes[what](n)
        if i > AHEAD:
            forward_group(i - AHEAD)

    high, total, weighted = stats
    inverse = 1.0 / total
    delta = weighted * inverse

    def backward(items):
        sources = [source(item) for item in items]
        scaled = []
        for item, (_, _, base, _) in zip(items, sources):
            factor = jnp.exp2(mbuf[slot(item)][:1] - high) * inverse
            scaled.append(ebuf[base, :] * factor)
        w = jnp.concatenate(scaled, axis=0)
        dp = jnp.concatenate([dpbuf[base, :] for _, _, base, _ in sources], axis=0)
        wb = w.astype(BF16)
        ds = (w * (dp - delta)).astype(BF16)
        dk = (dot(ds, qs[...], 1, 0) * scale).astype(BF16)
        dv = dot(wb, dos[...], 1, 0).astype(BF16)
        done = 0
        for item, (buffer, at_rows, base, _) in zip(items, sources):
            now = slice(done, done + base.size)
            done += base.size
            wbuf[base, :] = wb[now]
            dsbuf[base, :] = ds[now]
            own, received, send, arrived = grads(item)
            own[0, at_rows] = dk[now]
            own[1, at_rows] = dv[now]
            copy_to(own.at[other, at_rows], received.at[at_rows], send, arrived, mate)

    def grads(item):
        what, n = item
        if what == "w":
            return gw, gwin, gwx_send, gwx_recv.at[n]
        return gp, gpin, gx_send, gx_recv.at[index_a(n) if what == "a" else GROUP + index_b(n)]

    def both_cores(rows_at, arrived):
        wait_bytes(gpin.at[rows_at], arrived)
        total = gp[kind, rows_at].astype(F32) + gpin[rows_at, :].astype(F32)
        gpout[rows_at, :] = total.astype(BF16)

    def send_piece(index, to):
        @pl.when(to != me)
        def _():
            copy_to(gpout.at[at(index, plocal)], rs.at[me], rs_send, rs_recv, {"resp": to})

    def finish_a(bz):
        pz = index_a(bz)
        both_cores(part_a(pz), gx_recv.at[pz])
        for j in range(ny // 2):
            place = lax.rem(y // 2 + j, ny // 2)
            send_piece(pz * (ny // 2) + place, (2 * place + lax.rem(pz, 2)) * GROUP + pz)

    def send_b(by, place):
        py = index_b(by)
        to = py * GROUP + 2 * place + 1 - lax.rem(py, 2)
        send_piece(GROUP * (ny // 2) + py * (GROUP // 2) + place, to)

    def finish_b(by):
        py = index_b(by)
        both_cores(part_b(py), gx_recv.at[GROUP + py])
        send_b(by, 0)
        send_b(by, 1)

    def finish_window(off):
        wait_bytes(gwin.at[block(off)], gwx_recv.at[off])
        both = gw[kind, block(off)].astype(F32) + gwin[block(off), :].astype(F32)
        if isinstance(off, int) and off == 0:
            return both
        gwout[block(off), :] = both.astype(BF16)
        size = block(off).size
        copy_to(
            gwout.at[block(off)], wr.at[off - 1, pl.ds(0, size)], wr_send, wr_recv.at[off - 1],
            peer(-off),
        )
        return None

    finishes = {"a": finish_a, "b": finish_b, "w": finish_window}

    def ring(r):
        return ("a", lax.rem(r - z + GROUP, GROUP))

    def columns(parity):
        return [
            ("b", lax.rem(2 * lax.rem(y // 2 + j, ny // 2) + parity - y + ny, ny))
            for j in range(ny // 2)
        ]

    def nearest(r):
        return ("w", lax.rem(z - r + GROUP - 1, GROUP) + 1)

    def in_pairs(items):
        return [items[i : i + 2] for i in range(0, len(items), 2)]

    def send_rest(parity):
        for _, by in columns(parity):
            send_b(by, 1)

    far = [("w", off) for off in range(GROUP + 1, reach + 1)]
    back = [[nearest(0)] + far, [nearest(1)], [("a", 2)]]
    spread = in_pairs([("b", by) for by in y_order[::-1]])
    back += spread[:2] + [[("a", 1)], [nearest(2)], [("a", 3)]] + spread[2:]
    rest = {}
    back += [[nearest(3)], [("b", 0), ("a", 0)], [("w", 0)]]
    for i in range(len(back) + BEHIND):
        if i < len(back):
            backward(back[i])
        if i >= BEHIND:
            for what, n in back[i - BEHIND]:
                own_grad = finishes[what](n)
            if i - BEHIND in rest:
                send_rest(rest[i - BEHIND])
    rs[me] = gpout[own_p, :]

    p_part = pl.ds(0, total_p)
    w_part = pl.ds(total_p, ahead + rows)
    out_t = dot(kvp[1], wbuf[p_part, :], 0, 0) + dot(kvw[1], wbuf[w_part, :], 0, 0)
    out = out_t.T.astype(BF16)
    for h in range(heads):
        att_ref[:, h * d : (h + 1) * d] = out[h * rows : (h + 1) * rows]
    dq_t = dot(kvp[0], dsbuf[p_part, :], 0, 0) + dot(kvw[0], dsbuf[w_part, :], 0, 0)
    dq = (dq_t.T * scale).astype(BF16)
    for h in range(heads):
        dq_ref[:, h * d : (h + 1) * d] = dq[h * rows : (h + 1) * rows]

    for off in range(1, reach):
        wait_bytes(wr.at[off - 1], wr_recv.at[off - 1])
        own_grad = own_grad + wr[off - 1].astype(F32)
    far = wr.at[reach - 1, pl.ds(0, tail)]
    wait_bytes(far, wr_recv.at[reach - 1])
    own_grad = jnp.concatenate(
        [own_grad[: rows - tail], own_grad[rows - tail :] + far[...].astype(F32)], axis=0
    )
    dkv_ref[...] = own_grad.astype(BF16)
    wait_bytes(rs.at[pl.ds(0, count - 1)], rs_recv)
    dpkv_ref[...] = jnp.sum(rs[...].astype(F32), axis=0).astype(BF16)

    @pl.when(odd == 0)
    def _():
        wait_bytes(kvp.at[0, pl.ds(0, (ny - 1) * plocal)], one_send.at[0])

    @pl.when(odd == 1)
    def _():
        wait_bytes(kvp.at[0, pl.ds(0, (GROUP - 1) * plocal)], one_send.at[1])

    wait_bytes(kvp.at[0, pl.ds(0, (GROUP - 1) * size_a + (ny - 1) * size_b)], two_send)
    wait_bytes(kvp.at[0], pf_send)
    wait_bytes(kvw.at[0, pl.ds(0, ahead)], w_send)
    wait_bytes(kvw.at[0], wf_send)
    wait_bytes(gpin, gx_send)
    wait_bytes(gwin, gwx_send)
    wait_bytes(rs.at[pl.ds(0, count - 1)], rs_send)
    wait_bytes(gwout.at[pl.ds(0, ahead)], wr_send)


def shards(queries, response_key_value, prompt_key_value, output_cotangent, lengths):
    rows, width = queries.shape
    d = response_key_value.shape[1]
    cols = width // d * rows
    plocal = prompt_key_value.shape[0]
    count = lax.axis_size("resp")
    total_p = plocal * count
    ny = count // GROUP
    reach, tail = window_shape(rows)
    window = tail + reach * rows
    keys = total_p + window
    dma, anywhere = pltpu.SemaphoreType.DMA, pl.BlockSpec(memory_space=pl.ANY)
    whole = pl.BlockSpec(memory_space=pltpu.VMEM)
    limit = 60 * 1024 * 1024
    out_shape = (
        jax.ShapeDtypeStruct(queries.shape, BF16),
        jax.ShapeDtypeStruct(queries.shape, BF16),
        jax.ShapeDtypeStruct(response_key_value.shape, BF16),
        jax.ShapeDtypeStruct(prompt_key_value.shape, BF16),
    )
    results = pl.pallas_call(
        functools.partial(kernel, count),
        out_shape=tuple(pltpu.VMEM(s.shape, s.dtype) for s in out_shape),
        in_specs=[anywhere] * 4 + [pl.BlockSpec(memory_space=pltpu.SMEM)],
        out_specs=(whole,) * 4,
        scratch_shapes=[
            pltpu.VMEM((cols, d), BF16),
            pltpu.VMEM((cols, d), BF16),
            pltpu.VMEM((2, total_p, d), BF16),
            pltpu.VMEM((2, window, d), BF16),
            pltpu.VMEM((keys, cols), F32),
            pltpu.VMEM((keys, cols), F32),
            pltpu.VMEM((GROUP + ny + reach + 1, 8, cols), F32),
            pltpu.VMEM((keys, cols), BF16),
            pltpu.VMEM((keys, cols), BF16),
            pltpu.VMEM((2, total_p, d), BF16),
            pltpu.VMEM((total_p, d), BF16),
            pltpu.VMEM((total_p, d), BF16),
            pltpu.VMEM((count, plocal, d), BF16),
            pltpu.VMEM((2, window, d), BF16),
            pltpu.VMEM((window, d), BF16),
            pltpu.VMEM((window, d), BF16),
            pltpu.VMEM((reach, rows, d), BF16),
            dma((3,)), dma, dma((2,)), dma((ny // 2,)), dma((GROUP // 2,)), dma, dma((GROUP,)),
            dma((ny,)),
            dma, dma((GROUP + ny,)),
            dma, dma((reach,)), dma, dma((reach + 1,)),
            dma, dma((GROUP + ny,)), dma, dma((reach + 1,)),
            dma, dma, dma, dma((reach,)),
        ],
        compiler_params=pltpu.CompilerParams(
            collective_id=0, has_side_effects=True, vmem_limit_bytes=limit
        ),
    )(queries, response_key_value, prompt_key_value, output_cotangent, lengths)
    return pl.pallas_call(
        copy_kernel,
        out_shape=out_shape,
        in_specs=[whole] * 4,
        out_specs=(whole,) * 4,
        compiler_params=pltpu.CompilerParams(vmem_limit_bytes=limit),
    )(*[pltpu.with_memory_space_constraint(r, pltpu.VMEM) for r in results])


def solution(mesh):
    spec = P("resp", "head")
    return jax.shard_map(
        shards,
        mesh=mesh,
        in_specs=(spec, spec, spec, spec, P()),
        out_specs=(spec, spec, spec, spec),
        check_vma=False,
    )
```
